1024 devices in a mesh: row: 32 (over y_lo, x, core), col: 32 (over y_hi, z).
Axes of the slice: x: 4, y: 8 (y_hi: 2, y_lo: 4; y = y_hi * 4 + y_lo), z: 16, core: 2. Of those that a mesh axis runs over, the one named last changes fastest.
Arguments:
- stored: bfloat16 [32, 32, 32, 128, 128], P('row', 'col'), may hold values from -3 to 3, as said below
- pair_rows: int32 [32, 32, 32, 2, 2], P('row', 'col'), may hold values from 0 to 2047, as said below
- pair_cols: int32 [32, 32, 32, 2, 2], P('row', 'col'), may hold values from 0 to 2047, as said below
- block_owner: int32 [2048], replicated, may hold values from 0 to 2047, as said below
Outputs:
- window: float32 [32, 32, 32, 128, 128], P('row', 'col')
The draws below stay inside these ranges and needn't reach their ends.
Inputs may be any that keep to these rules, and one draw needn't show every extreme that they name: A permutation of the block indices; block g lies at grid row block_owner[g] // 64, grid column (block_owner[g] // 2) % 32, place block_owner[g] % 2. `pair_rows`: entry [r, c, y, a, b] is the block index at grid row r, grid column y, place a. `pair_cols`: entry [r, c, y, a, b] is the block index at grid row p, grid column c, place b, where p = (r + q[c] - q[y]) mod 32 for a one-to-one q from grid columns to grid rows; so the row group at (r, y) is coupled, densely, to exactly one group of each grid column, these lie in distinct grid rows, and the coupling is symmetric. `stored`: zero on every 64 x 64 block whose pair_rows exceeds its pair_cols; blocks with equal row and column index are symmetric.
All inputs are finite; a program needn't handle non-finite values.
Results may differ from the reference program's by a relative error of at most 0.0003.
Values may be sent and summed in bfloat16 or wider, within the bound.
A program may use at most 32 MiB of HBM per device.

```python
import jax
import jax.numpy as jnp

BLK = 64
TB = 2
N_ROW = 32
N_COL = 32


def layout(key):
    count_all = N_ROW * N_COL * TB
    owner_map = jax.random.permutation(jax.random.fold_in(key, 101), count_all).astype(jnp.int32)
    inverse = jnp.zeros((count_all,), jnp.int32).at[owner_map].set(jnp.arange(count_all, dtype=jnp.int32))
    column_rows = jax.random.permutation(jax.random.fold_in(key, 102), N_ROW).astype(jnp.int32)[:N_COL]
    grid_row = jnp.arange(N_ROW, dtype=jnp.int32)[:, None, None]
    grid_col = jnp.arange(N_COL, dtype=jnp.int32)[None, :, None]
    slot_index = jnp.arange(N_COL, dtype=jnp.int32)[None, None, :]
    partner = (grid_row + column_rows[grid_col] - column_rows[slot_index]) % N_ROW
    place_row = jnp.arange(TB, dtype=jnp.int32)[:, None]
    place_col = jnp.arange(TB, dtype=jnp.int32)[None, :]
    full_shape = (N_ROW, N_COL, N_COL, TB, TB)
    row_pos = jnp.broadcast_to(((grid_row * N_COL + slot_index) * TB)[..., None, None] + place_row, full_shape)
    col_pos = jnp.broadcast_to(((partner * N_COL + grid_col) * TB)[..., None, None] + place_col, full_shape)
    return (owner_map, inverse[row_pos], inverse[col_pos])


def draw_block_owner(key, part):
    owner_map, row_ids, col_ids = layout(key)
    return owner_map


def draw_pair_rows(key, part):
    owner_map, row_ids, col_ids = layout(key)
    return row_ids


def draw_pair_cols(key, part):
    owner_map, row_ids, col_ids = layout(key)
    return col_ids


def draw_stored(key, part):
    owner_map, row_ids, col_ids = layout(key)
    key = jax.random.fold_in(key, 9)
    sample_shape = (N_ROW, N_COL, N_COL, TB, BLK, TB, BLK)
    samples = 0.25 * jax.random.normal(key, sample_shape, jnp.float32)
    flipped = jnp.swapaxes(samples, 4, 6)
    on_diagonal = (row_ids == col_ids)[:, :, :, :, None, :, None]
    kept_mask = (row_ids <= col_ids)[:, :, :, :, None, :, None]
    symmetric = jnp.where(on_diagonal, 0.7071 * (samples + flipped), samples)
    entries = jnp.where(kept_mask, symmetric, 0.0)
    return entries.reshape(N_ROW, N_COL, N_COL, TB * BLK, TB * BLK).astype(jnp.bfloat16)


def setup_inputs(seed: int = 0) -> dict:
    arg_keys = jax.random.split(jax.random.key(seed), 5)
    stored = draw_stored(jax.random.fold_in(arg_keys[4], 71), 0)
    pair_rows = draw_pair_rows(jax.random.fold_in(arg_keys[4], 71), 0)
    pair_cols = draw_pair_cols(jax.random.fold_in(arg_keys[4], 71), 0)
    block_owner = draw_block_owner(jax.random.fold_in(arg_keys[4], 71), 0)
    return {"stored": stored, "pair_rows": pair_rows, "pair_cols": pair_cols, "block_owner": block_owner}


def reference(stored, pair_rows, pair_cols, block_owner):
    partner = block_owner[pair_cols[:, :, :, 0, 0]] // (N_COL * TB)
    strict = pair_rows < pair_cols
    mask = jnp.repeat(jnp.repeat(strict, BLK, axis=3), BLK, axis=4)
    upper = jnp.where(mask, stored, jnp.zeros_like(stored))
    grid_col = jnp.arange(N_COL, dtype=jnp.int32)[None, :, None]
    slot_index = jnp.arange(N_COL, dtype=jnp.int32)[None, None, :]
    mirrored = upper[partner, slot_index, grid_col]
    complete = stored + jnp.swapaxes(mirrored, 3, 4)
    following = (grid_col + 1) % N_COL
    next_cols = (jnp.arange(N_COL, dtype=jnp.int32) + 1) % N_COL
    diag_blocks = complete[partner, grid_col, grid_col]
    ahead_partner = partner[:, next_cols, :]
    ahead_tile = complete[:, next_cols]
    ahead_blocks = complete[ahead_partner, grid_col, following]
    diag_term = jnp.einsum("rcyab,rcybd->rcyad", complete.astype(jnp.float32), diag_blocks.astype(jnp.float32))
    ahead_term = jnp.einsum("rcyab,rcybd->rcyad", ahead_tile.astype(jnp.float32), ahead_blocks.astype(jnp.float32))
    return diag_term + ahead_term
```

```python
import functools

import jax
import jax.numpy as jnp
from jax import lax
from jax.experimental import pallas as pl
from jax.experimental.pallas import tpu as pltpu
from jax.sharding import PartitionSpec as P

MESH = pl.DeviceIdType.MESH

ROW_SPLIT = (4, 4, 2)
COL_SPLIT = (2, 16)
CHUNKS = 4


def kernel(
    row_split, col_split, chunks, jc_ref, inv_ref, stored_ref, out_ref, turned, gathered, ahead, total, total_next, *rest
):
    landed, buckets, mirrored = rest[:chunks], rest[chunks : 2 * chunks], rest[2 * chunks : 3 * chunks]
    send_sem, m_sem, g_sem, a_sem, b_sem, w_sem = rest[3 * chunks :]
    ny, nx, ncore = row_split
    nhi, nz = col_split
    nr, nc = ny * nx * ncore, nhi * nz
    width = stored_ref.shape[-1]
    strip = width // chunks
    r, c = lax.axis_index("row"), lax.axis_index("col")
    core, x, y = lax.rem(r, ncore), lax.rem(r // ncore, nx), r // (ncore * nx)
    z, hi = lax.rem(c, nz), c // nz
    following, previous = lax.rem(c + 1, nc), lax.rem(c + nc - 1, nc)

    def remote(src, dst, slot, recv, **where):
        return pltpu.make_async_remote_copy(
            src_ref=src,
            dst_ref=dst,
            send_sem=send_sem.at[slot],
            recv_sem=recv,
            device_id=where,
            device_id_type=MESH,
        )

    barrier = pltpu.get_barrier_semaphore()

    def greet_col(t, carry):
        pl.semaphore_signal(barrier, inc=1, device_id={"col": lax.rem(c + t, nc)}, device_id_type=MESH)
        return carry

    def greet_row(t, carry):
        pl.semaphore_signal(barrier, inc=1, device_id={"row": lax.rem(r + t, nr)}, device_id_type=MESH)
        return carry

    lax.fori_loop(1, nc, greet_col, 0)
    lax.fori_loop(1, nr, greet_row, 0)

    def turn(t, carry):
        turned[t] = stored_ref[t].T
        return carry

    lax.fori_loop(0, nc, turn, 0, unroll=2)

    half = width // 2
    rows = lax.broadcasted_iota(jnp.int32, (width, width), 0)
    cols = lax.broadcasted_iota(jnp.int32, (width, width), 1)
    own = stored_ref[c].astype(jnp.float32)
    flipped = turned[c].astype(jnp.float32)
    diagonal = (own + jnp.where((rows >= half) != (cols >= half), flipped, 0.0)).astype(jnp.bfloat16)
    gathered[y, x, core, 0] = diagonal
    gathered[y, x, core, 1] = stored_ref[following]
    total[0] = diagonal

    pl.semaphore_wait(barrier, nc + nr - 2)

    ahead_copy = remote(
        turned.at[previous], gathered.at[y, x, core, 2], 0, m_sem.at[0], col=previous
    )
    ahead_copy.start()

    def offset_col(t):
        m = t // nhi
        sign = 2 * lax.rem(m, 2) - 1
        return lax.rem(hi + lax.rem(t, nhi), nhi) * nz + lax.rem(z + sign * ((m + 1) // 2) + nz, nz)

    for k in range(chunks):
        rows_k = pl.ds(k * strip, strip)

        def send_col(s, carry, k=k, rows_k=rows_k):
            to = offset_col(nc - s)
            remote(turned.at[to, rows_k], landed[k].at[c], 1, a_sem.at[k], col=to).start()
            return carry

        lax.fori_loop(1, nc, send_col, 0)

    ahead_copy.wait_recv()
    mine = gathered.at[y, x, core]
    for s in range(1, ny):
        remote(mine, mine, 4 + s, g_sem.at[s], row=(lax.rem(y + s, ny) * nx + x) * ncore + core).start()

    def gather_x():
        for s in range(1, ny):
            remote(mine, mine, 4 + s, g_sem.at[s], row=r).wait_recv()
        line = gathered.at[:, x, core]
        for s in range(1, nx):
            remote(line, line, 4 + ny + s, g_sem.at[ny + s], row=(y * nx + lax.rem(x + s, nx)) * ncore + core).start()

    def gather_core():
        line = gathered.at[:, x, core]
        for s in range(1, nx):
            remote(line, line, 4 + ny + s, g_sem.at[ny + s], row=r).wait_recv()
        plane = gathered.at[:, :, core]
        for s in range(1, ncore):
            remote(plane, plane, 4 + ny + nx + s, g_sem.at[ny + nx + s], row=(y * nx + x) * ncore + lax.rem(core + s, ncore)).start()

    for k in range(chunks):
        rows_k = pl.ds(k * strip, strip)
        remote(landed[k].at[pl.ds(1, nc - 1)], landed[k].at[pl.ds(1, nc - 1)], 1, a_sem.at[k], row=r).wait_recv()

        def send_row(t, carry, k=k):
            j = nr // 2 + (2 * lax.rem(t, 2) - 1) * ((t + 1) // 2)
            buckets[k][j] = landed[k][inv_ref[j]]
            remote(buckets[k].at[j], mirrored[k].at[j], 2, b_sem.at[k], row=lax.rem(r + j, nr)).start()
            return carry

        lax.fori_loop(0, nr - 1, send_row, 0)
        if k == 0:
            gather_x()
        if k == min(1, chunks - 1):
            gather_core()
        remote(mirrored[k].at[pl.ds(1, nr - 1)], mirrored[k].at[pl.ds(1, nr - 1)], 2, b_sem.at[k], row=r).wait_recv()

        def complete(j, carry, k=k, rows_k=rows_k):
            total[j, rows_k] = stored_ref[inv_ref[j], rows_k] + mirrored[k][j]
            return carry

        lax.fori_loop(1, nr, complete, 0)
        remote(total.at[:, rows_k], total_next.at[:, rows_k], 3, w_sem.at[k], col=previous).start()

    plane = gathered.at[:, :, core]
    for s in range(1, ncore):
        remote(plane, plane, 4 + ny + nx + s, g_sem.at[ny + nx + s], row=r).wait_recv()
    shift = jc_ref[following]

    def place(row):
        row = lax.rem(row + 2 * nr, nr)
        return row // (ncore * nx), lax.rem(row // ncore, nx), lax.rem(row, ncore)

    def fill_ahead(p, carry):
        here, there = place(p), place(p - shift)
        ahead[p] = gathered[here[0], here[1], here[2], 1] + gathered[there[0], there[1], there[2], 2]
        return carry

    lax.fori_loop(0, nr, fill_ahead, 0)

    def diag_term(t, carry):
        j = jc_ref[t]
        at = place(r - j)
        out_ref[t] = jnp.dot(total[j], gathered[at[0], at[1], at[2], 0], preferred_element_type=jnp.float32)
        return carry

    lax.fori_loop(0, nc, diag_term, 0, unroll=2)
    for k in range(chunks):
        rows_k = pl.ds(k * strip, strip)
        remote(total.at[:, rows_k], total_next.at[:, rows_k], 3, w_sem.at[k], col=previous).wait_recv()

    def ahead_term(t, carry):
        j = lax.rem(jc_ref[t] - shift + nr, nr)
        out_ref[t] += jnp.dot(
            total_next[j], ahead[lax.rem(r - j + nr, nr)], preferred_element_type=jnp.float32
        )
        return carry

    lax.fori_loop(0, nc, ahead_term, 0, unroll=2)

    ahead_copy.wait_send()
    remote(turned.at[pl.ds(1, nc - 1)], turned.at[pl.ds(1, nc - 1)], 1, m_sem.at[0], row=r).wait_send()
    for s in range(1, ny):
        remote(mine, mine, 4 + s, g_sem.at[s], row=r).wait_send()
    line = gathered.at[:, x, core]
    for s in range(1, nx):
        remote(line, line, 4 + ny + s, g_sem.at[ny + s], row=r).wait_send()
    for s in range(1, ncore):
        remote(plane, plane, 4 + ny + nx + s, g_sem.at[ny + nx + s], row=r).wait_send()
    remote(turned.at[pl.ds(1, nr - 1)], turned.at[pl.ds(1, nr - 1)], 2, m_sem.at[0], row=r).wait_send()
    remote(total, total, 3, m_sem.at[0], row=r).wait_send()


def body(row_split, col_split, chunks, stored, pair_rows, pair_cols, block_owner):
    nr, nc = lax.axis_size("row"), lax.axis_size("col")
    places = pair_rows.shape[-1]
    width = stored.shape[-1]
    strip = width // chunks
    partner = block_owner[pair_cols[0, 0, :, 0, 0]] // (nc * places)
    jc = lax.rem(lax.axis_index("row") - partner + nr, nr)
    slots = lax.broadcasted_iota(jnp.int32, (nr, nc), 1)
    inv = jnp.sum(jnp.where(jc[None, :] == jnp.arange(nr, dtype=jnp.int32)[:, None], slots, 0), axis=1)
    groups = jax.ShapeDtypeStruct((nc, width, width), jnp.bfloat16)
    vmem = lambda *shape: pltpu.VMEM(shape, jnp.bfloat16)
    smem_spec = pl.BlockSpec(memory_space=pltpu.SMEM)
    vmem_spec = pl.BlockSpec(memory_space=pltpu.VMEM)
    out = pl.pallas_call(
        functools.partial(kernel, row_split, col_split, chunks),
        out_shape=jax.ShapeDtypeStruct((nc, width, width), jnp.float32),
        in_specs=[smem_spec, smem_spec, vmem_spec],
        out_specs=vmem_spec,
        scratch_shapes=[
            vmem(nc, width, width),
            vmem(*row_split, 3, width, width),
            vmem(nr, width, width),
            vmem(nr, width, width),
            vmem(nr, width, width),
            *[vmem(nc, strip, width) for _ in range(chunks)],
            *[vmem(nr, strip, width) for _ in range(chunks)],
            *[vmem(nr, strip, width) for _ in range(chunks)],
            pltpu.SemaphoreType.DMA((4 + sum(row_split),)),
            pltpu.SemaphoreType.DMA((1,)),
            pltpu.SemaphoreType.DMA((sum(row_split),)),
            pltpu.SemaphoreType.DMA((chunks,)),
            pltpu.SemaphoreType.DMA((chunks,)),
            pltpu.SemaphoreType.DMA((chunks,)),
        ],
        compiler_params=pltpu.CompilerParams(
            collective_id=0, has_side_effects=True, vmem_limit_bytes=40 * 1024 * 1024
        ),
    )(jc, inv, stored[0, 0])
    return out[None, None]


def build(mesh, row_split, col_split, chunks):
    in_specs = (
        P("row", "col", None, None, None),
        P("row", "col", None, None, None),
        P("row", "col", None, None, None),
        P(),
    )
    out_specs = P("row", "col", None, None, None)
    run = functools.partial(body, row_split, col_split, chunks)
    return jax.shard_map(run, mesh=mesh, in_specs=in_specs, out_specs=out_specs, check_vma=False)


def solution(mesh):
    return build(mesh, ROW_SPLIT, COL_SPLIT, CHUNKS)
```

```python
import functools

import jax
import jax.numpy as jnp
from jax import lax
from jax.experimental import pallas as pl
from jax.experimental.pallas import tpu as pltpu
from jax.sharding import PartitionSpec as P

MESH = pl.DeviceIdType.MESH

ROW_SPLIT = (4, 4, 2)
COL_SPLIT = (2, 16)
STRIPS = (32, 32, 32, 32)
CROSSINGS = ((15, 8), (14, 8), (13, 8), (12, 8))


def kernel(
    row_split, col_split, strips, crossings, jc_ref, inv_ref, stored_ref, out_ref, turned, gathered, ahead, total, total_next, relayed, *rest
):
    chunks = len(strips)
    starts = [sum(strips[:k]) for k in range(chunks)]
    landed, buckets, mirrored = rest[:chunks], rest[chunks : 2 * chunks], rest[2 * chunks : 3 * chunks]
    send_sem, m_sem, g_sem, a_sem, b_sem, w_sem, r_sem = rest[3 * chunks :]
    ny, nx, ncore = row_split
    nhi, nz = col_split
    nr, nc = ny * nx * ncore, nhi * nz
    width = stored_ref.shape[-1]
    r, c = lax.axis_index("row"), lax.axis_index("col")
    core, x, y = lax.rem(r, ncore), lax.rem(lax.div(r, ncore), nx), lax.div(r, ncore * nx)
    z, hi = lax.rem(c, nz), lax.div(c, nz)
    following, previous = lax.rem(c + 1, nc), lax.rem(c + nc - 1, nc)

    def remote(src, dst, slot, recv, **where):
        return pltpu.make_async_remote_copy(
            src_ref=src,
            dst_ref=dst,
            send_sem=send_sem.at[slot],
            recv_sem=recv,
            device_id=where,
            device_id_type=MESH,
        )

    barrier = pltpu.get_barrier_semaphore()

    def greet_col(t, carry):
        pl.semaphore_signal(barrier, inc=1, device_id={"col": lax.rem(c + t, nc)}, device_id_type=MESH)
        return carry

    def greet_row(t, carry):
        pl.semaphore_signal(barrier, inc=1, device_id={"row": lax.rem(r + t, nr)}, device_id_type=MESH)
        return carry

    lax.fori_loop(1, nc, greet_col, 0)
    lax.fori_loop(1, nr, greet_row, 0)

    def turn(t, carry):
        turned[t] = stored_ref[t].T
        return carry

    lax.fori_loop(0, nc, turn, 0, unroll=2)

    half = width // 2
    rows = lax.broadcasted_iota(jnp.int32, (width, width), 0)
    cols = lax.broadcasted_iota(jnp.int32, (width, width), 1)
    own = stored_ref[c].astype(jnp.float32)
    flipped = turned[c].astype(jnp.float32)
    diagonal = (own + jnp.where((rows >= half) != (cols >= half), flipped, 0.0)).astype(jnp.bfloat16)
    gathered[y, x, core, 0] = diagonal
    gathered[y, x, core, 1] = stored_ref[following]
    total[0] = diagonal

    pl.semaphore_wait(barrier, nc + nr - 2)

    ahead_copy = remote(
        turned.at[previous], gathered.at[y, x, core, 2], 0, m_sem.at[0], col=previous
    )
    ahead_copy.start()

    here, other = hi * nz, (nhi - 1 - hi) * nz
    far = nz // 2

    def send_to(k, to):
        rows_k = pl.ds(starts[k], strips[k])
        remote(turned.at[to, rows_k], landed[k].at[c], 1, a_sem.at[k], col=to).start()

    def send_cols(k):
        up, down = lax.rem(z + far - 1, nz), lax.rem(z + far + 1, nz)
        send_to(k, here + lax.rem(z + far, nz))
        send_to(k, other + lax.rem(z + far, nz))
        send_to(k, here + down)
        send_to(k, here + up)
        send_to(k, other + down)
        send_to(k, other + up)

        def send_pairs(s, carry):
            m = far - s
            up, down = lax.rem(z + m, nz), lax.rem(z + nz - m, nz)
            send_to(k, here + up)
            send_to(k, other + down)
            send_to(k, other + up)
            send_to(k, here + down)
            return carry

        lax.fori_loop(2, far, send_pairs, 0)
        send_to(k, other + z)

    send_cols(0)
    ahead_copy.wait_recv()
    mine = gathered.at[y, x, core]
    for s in range(1, ny):
        remote(mine, mine, 7 + s, g_sem.at[s], row=(lax.rem(y + s, ny) * nx + x) * ncore + core).start()

    for k in range(1, chunks):
        send_cols(k)

    def gather_x():
        for s in range(1, ny):
            remote(mine, mine, 7 + s, g_sem.at[s], row=r).wait_recv()
        line = gathered.at[:, x, core]
        for s in range(1, nx):
            remote(line, line, 7 + ny + s, g_sem.at[ny + s], row=(y * nx + lax.rem(x + s, nx)) * ncore + core).start()

    def gather_core():
        line = gathered.at[:, x, core]
        for s in range(1, nx):
            remote(line, line, 7 + ny + s, g_sem.at[ny + s], row=r).wait_recv()
        plane = gathered.at[:, :, core]
        for s in range(1, ncore):
            remote(plane, plane, 7 + ny + nx + s, g_sem.at[ny + nx + s], row=(y * nx + x) * ncore + lax.rem(core + s, ncore)).start()

    def parts():
        start = 0
        for plane, count in crossings:
            yield plane, pl.ds(start, count), pl.ds(0, count)
            start += count

    def shift_on(k):
        rows_k = pl.ds(starts[k], strips[k])

        @pl.when(z != 0)
        def _():
            remote(total.at[:, rows_k], total_next.at[:, rows_k], 3, w_sem.at[k], col=previous).start()

        @pl.when(z == 0)
        def _():
            for plane, part, slots in parts():
                to = lax.rem(hi + nhi - 1, nhi) * nz + plane
                if plane == nz - 1:
                    dst, sem = total_next.at[part, rows_k], w_sem.at[k]
                else:
                    dst, sem = relayed.at[slots, rows_k], r_sem.at[k]
                remote(total.at[part, rows_k], dst, 3, sem, col=to).start()

    def relay_on(k):
        rows_k = pl.ds(starts[k], strips[k])
        for plane, part, slots in parts():
            if plane != nz - 1:

                @pl.when(z == plane)
                def _(part=part, slots=slots):
                    src, dst = relayed.at[slots, rows_k], total_next.at[part, rows_k]
                    remote(src, src, 3, r_sem.at[k], row=r).wait_recv()
                    remote(src, dst, 5, w_sem.at[k], col=hi * nz + nz - 1).start()

    for k in range(chunks):
        rows_k = pl.ds(starts[k], strips[k])
        remote(landed[k].at[pl.ds(1, nc - 1)], landed[k].at[pl.ds(1, nc - 1)], 1, a_sem.at[k], row=r).wait_recv()

        def send_row(j, k=k):
            buckets[k][j] = landed[k][inv_ref[j]]
            remote(buckets[k].at[j], mirrored[k].at[j], 2, b_sem.at[k], row=lax.rem(r + j, nr)).start()

        def send_rows(s, carry):
            send_row(nr // 2 - s)
            send_row(nr // 2 + s)
            return carry

        send_row(nr // 2)
        lax.fori_loop(1, nr // 2, send_rows, 0)
        if k == 0:
            gather_x()
        if k == min(1, chunks - 1):
            gather_core()
        if k > 0:
            relay_on(k - 1)
        remote(mirrored[k].at[pl.ds(1, nr - 1)], mirrored[k].at[pl.ds(1, nr - 1)], 2, b_sem.at[k], row=r).wait_recv()

        def complete(j, carry, k=k, rows_k=rows_k):
            total[j, rows_k] = stored_ref[inv_ref[j], rows_k] + mirrored[k][j]
            return carry

        lax.fori_loop(1, nr, complete, 0)
        shift_on(k)

    relay_on(chunks - 1)
    plane = gathered.at[:, :, core]
    for s in range(1, ncore):
        remote(plane, plane, 7 + ny + nx + s, g_sem.at[ny + nx + s], row=r).wait_recv()
    shift = jc_ref[following]

    def place(row):
        row = lax.rem(row + 2 * nr, nr)
        return lax.div(row, ncore * nx), lax.rem(lax.div(row, ncore), nx), lax.rem(row, ncore)

    def fill_ahead(p, carry):
        here, there = place(p), place(p - shift)
        ahead[p] = gathered[here[0], here[1], here[2], 1] + gathered[there[0], there[1], there[2], 2]
        return carry

    lax.fori_loop(0, nr, fill_ahead, 0)

    def diag_term(t, carry):
        j = jc_ref[t]
        at = place(r - j)
        out_ref[t] = jnp.dot(total[j], gathered[at[0], at[1], at[2], 0], preferred_element_type=jnp.float32)
        return carry

    lax.fori_loop(0, nc, diag_term, 0, unroll=2)
    for k in range(chunks):
        rows_k = pl.ds(starts[k], strips[k])
        remote(total.at[:, rows_k], total_next.at[:, rows_k], 3, w_sem.at[k], col=previous).wait_recv()

    def ahead_term(t, carry):
        j = lax.rem(jc_ref[t] - shift + nr, nr)
        out_ref[t] += jnp.dot(
            total_next[j], ahead[lax.rem(r - j + nr, nr)], preferred_element_type=jnp.float32
        )
        return carry

    lax.fori_loop(0, nc, ahead_term, 0, unroll=2)

    ahead_copy.wait_send()
    sent = turned.at[pl.ds(0, nc - 1)]
    remote(sent, sent, 1, m_sem.at[0], row=r).wait_send()
    for s in range(1, ny):
        remote(mine, mine, 7 + s, g_sem.at[s], row=r).wait_send()
    line = gathered.at[:, x, core]
    for s in range(1, nx):
        remote(line, line, 7 + ny + s, g_sem.at[ny + s], row=r).wait_send()
    for s in range(1, ncore):
        remote(plane, plane, 7 + ny + nx + s, g_sem.at[ny + nx + s], row=r).wait_send()
    remote(turned.at[pl.ds(1, nr - 1)], turned.at[pl.ds(1, nr - 1)], 2, m_sem.at[0], row=r).wait_send()
    remote(total, total, 3, m_sem.at[0], row=r).wait_send()
    for between, _, slots in parts():
        if between != nz - 1:

            @pl.when(z == between)
            def _(slots=slots):
                remote(relayed.at[slots], relayed.at[slots], 5, m_sem.at[0], row=r).wait_send()


def body(row_split, col_split, strips, crossings, stored, pair_rows, pair_cols, block_owner):
    nr, nc = lax.axis_size("row"), lax.axis_size("col")
    places = pair_rows.shape[-1]
    width = stored.shape[-1]
    chunks = len(strips)
    partner = block_owner[pair_cols[0, 0, :, 0, 0]] // (nc * places)
    jc = lax.rem(lax.axis_index("row") - partner + nr, nr)
    slots = lax.broadcasted_iota(jnp.int32, (nr, nc), 1)
    inv = jnp.sum(jnp.where(jc[None, :] == jnp.arange(nr, dtype=jnp.int32)[:, None], slots, 0), axis=1)
    groups = jax.ShapeDtypeStruct((nc, width, width), jnp.bfloat16)
    vmem = lambda *shape: pltpu.VMEM(shape, jnp.bfloat16)
    smem_spec = pl.BlockSpec(memory_space=pltpu.SMEM)
    vmem_spec = pl.BlockSpec(memory_space=pltpu.VMEM)
    out = pl.pallas_call(
        functools.partial(kernel, row_split, col_split, strips, crossings),
        out_shape=jax.ShapeDtypeStruct((nc, width, width), jnp.float32),
        in_specs=[smem_spec, smem_spec, vmem_spec],
        out_specs=vmem_spec,
        scratch_shapes=[
            vmem(nc, width, width),
            vmem(*row_split, 3, width, width),
            vmem(nr, width, width),
            vmem(nr, width, width),
            vmem(nr, width, width),
            vmem(max(count for _, count in crossings), width, width),
            *[vmem(nc, strip, width) for strip in strips],
            *[vmem(nr, strip, width) for strip in strips],
            *[vmem(nr, strip, width) for strip in strips],
            pltpu.SemaphoreType.DMA((7 + sum(row_split),)),
            pltpu.SemaphoreType.DMA((1,)),
            pltpu.SemaphoreType.DMA((sum(row_split),)),
            pltpu.SemaphoreType.DMA((chunks,)),
            pltpu.SemaphoreType.DMA((chunks,)),
            pltpu.SemaphoreType.DMA((chunks,)),
            pltpu.SemaphoreType.DMA((chunks,)),
        ],
        compiler_params=pltpu.CompilerParams(
            collective_id=0, has_side_effects=True, vmem_limit_bytes=40 * 1024 * 1024
        ),
    )(jc, inv, stored[0, 0])
    return out[None, None]


def build(mesh, row_split, col_split, strips, crossings):
    in_specs = (
        P("row", "col", None, None, None),
        P("row", "col", None, None, None),
        P("row", "col", None, None, None),
        P(),
    )
    out_specs = P("row", "col", None, None, None)
    run = functools.partial(body, row_split, col_split, strips, crossings)
    return jax.shard_map(run, mesh=mesh, in_specs=in_specs, out_specs=out_specs, check_vma=False)


def solution(mesh):
    return build(mesh, ROW_SPLIT, COL_SPLIT, STRIPS, CROSSINGS)
```

```python
import functools

import jax
import jax.numpy as jnp
from jax import lax
from jax.experimental import pallas as pl
from jax.experimental.pallas import tpu as pltpu
from jax.sharding import PartitionSpec as P

MESH = pl.DeviceIdType.MESH

ROW_SPLIT = (4, 4, 2)
COL_SPLIT = (2, 16)
STRIPS = (32, 32, 32, 32)
CROSSINGS = ((15, 8), (14, 6), (13, 6), (12, 6), (11, 6))


def kernel(
    row_split, col_split, strips, crossings, jc_ref, inv_ref, stored_ref, out_ref, turned, gathered, ahead, total, total_next, relayed, *rest
):
    chunks = len(strips)
    starts = [sum(strips[:k]) for k in range(chunks)]
    landed, buckets, mirrored = rest[:chunks], rest[chunks : 2 * chunks], rest[2 * chunks : 3 * chunks]
    send_sem, m_sem, g_sem, a_sem, b_sem, w_sem, r_sem = rest[3 * chunks :]
    ny, nx, ncore = row_split
    nhi, nz = col_split
    nr, nc = ny * nx * ncore, nhi * nz
    width = stored_ref.shape[-1]
    r, c = lax.axis_index("row"), lax.axis_index("col")
    core, x, y = lax.rem(r, ncore), lax.rem(lax.div(r, ncore), nx), lax.div(r, ncore * nx)
    z, hi = lax.rem(c, nz), lax.div(c, nz)
    following, previous = lax.rem(c + 1, nc), lax.rem(c + nc - 1, nc)

    def remote(src, dst, slot, recv, **where):
        return pltpu.make_async_remote_copy(
            src_ref=src,
            dst_ref=dst,
            send_sem=send_sem.at[slot],
            recv_sem=recv,
            device_id=where,
            device_id_type=MESH,
        )

    barrier = pltpu.get_barrier_semaphore()

    def greet_col(t, carry):
        pl.semaphore_signal(barrier, inc=1, device_id={"col": lax.rem(c + t, nc)}, device_id_type=MESH)
        return carry

    def greet_row(t, carry):
        pl.semaphore_signal(barrier, inc=1, device_id={"row": lax.rem(r + t, nr)}, device_id_type=MESH)
        return carry

    lax.fori_loop(1, nc, greet_col, 0)
    lax.fori_loop(1, nr, greet_row, 0)

    def turn(t, carry):
        turned[t] = stored_ref[t].T
        return carry

    lax.fori_loop(0, nc, turn, 0, unroll=2)

    half = width // 2
    rows = lax.broadcasted_iota(jnp.int32, (width, width), 0)
    cols = lax.broadcasted_iota(jnp.int32, (width, width), 1)
    own = stored_ref[c].astype(jnp.float32)
    flipped = turned[c].astype(jnp.float32)
    diagonal = (own + jnp.where((rows >= half) != (cols >= half), flipped, 0.0)).astype(jnp.bfloat16)
    gathered[y, x, core, 0] = diagonal
    gathered[y, x, core, 1] = stored_ref[following]
    total[0] = diagonal

    pl.semaphore_wait(barrier, nc + nr - 2)

    ahead_copy = remote(
        turned.at[previous], gathered.at[y, x, core, 2], 0, m_sem.at[0], col=previous
    )
    ahead_copy.start()

    here, other = hi * nz, (nhi - 1 - hi) * nz
    far = nz // 2

    def send_to(k, to):
        rows_k = pl.ds(starts[k], strips[k])
        remote(turned.at[to, rows_k], landed[k].at[c], 1, a_sem.at[k], col=to).start()

    def send_cols(k):
        up, down = lax.rem(z + far - 1, nz), lax.rem(z + far + 1, nz)
        send_to(k, here + lax.rem(z + far, nz))
        send_to(k, other + lax.rem(z + far, nz))
        send_to(k, here + down)
        send_to(k, here + up)
        send_to(k, other + down)
        send_to(k, other + up)

        def send_pairs(s, carry):
            m = far - s
            up, down = lax.rem(z + m, nz), lax.rem(z + nz - m, nz)
            send_to(k, here + up)
            send_to(k, other + down)
            send_to(k, other + up)
            send_to(k, here + down)
            return carry

        lax.fori_loop(2, far, send_pairs, 0)
        send_to(k, other + z)

    send_cols(0)
    ahead_copy.wait_recv()
    mine = gathered.at[y, x, core]
    for s in range(1, ny):
        remote(mine, mine, 7 + s, g_sem.at[s], row=(lax.rem(y + s, ny) * nx + x) * ncore + core).start()

    for k in range(1, chunks):
        send_cols(k)

    def gather_x():
        for s in range(1, ny):
            remote(mine, mine, 7 + s, g_sem.at[s], row=r).wait_recv()
        line = gathered.at[:, x, core]
        for s in range(1, nx):
            remote(line, line, 7 + ny + s, g_sem.at[ny + s], row=(y * nx + lax.rem(x + s, nx)) * ncore + core).start()

    def gather_core():
        line = gathered.at[:, x, core]
        for s in range(1, nx):
            remote(line, line, 7 + ny + s, g_sem.at[ny + s], row=r).wait_recv()
        plane = gathered.at[:, :, core]
        for s in range(1, ncore):
            remote(plane, plane, 7 + ny + nx + s, g_sem.at[ny + nx + s], row=(y * nx + x) * ncore + lax.rem(core + s, ncore)).start()

    def parts():
        start = 0
        for plane, count in crossings:
            yield plane, pl.ds(start, count), pl.ds(0, count)
            start += count

    def shift_on(k):
        rows_k = pl.ds(starts[k], strips[k])

        @pl.when(z != 0)
        def _():
            remote(total.at[:, rows_k], total_next.at[:, rows_k], 3, w_sem.at[k], col=previous).start()

        @pl.when(z == 0)
        def _():
            for plane, part, slots in parts():
                to = lax.rem(hi + nhi - 1, nhi) * nz + plane
                if plane == nz - 1:
                    dst, sem = total_next.at[part, rows_k], w_sem.at[k]
                else:
                    dst, sem = relayed.at[slots, rows_k], r_sem.at[k]
                remote(total.at[part, rows_k], dst, 3, sem, col=to).start()

    def relay_on(k):
        rows_k = pl.ds(starts[k], strips[k])
        for plane, part, slots in parts():
            if plane != nz - 1:

                @pl.when(z == plane)
                def _(part=part, slots=slots):
                    src, dst = relayed.at[slots, rows_k], total_next.at[part, rows_k]
                    remote(src, src, 3, r_sem.at[k], row=r).wait_recv()
                    remote(src, dst, 5, w_sem.at[k], col=hi * nz + nz - 1).start()

    for k in range(chunks):
        rows_k = pl.ds(starts[k], strips[k])
        remote(landed[k].at[pl.ds(1, nc - 1)], landed[k].at[pl.ds(1, nc - 1)], 1, a_sem.at[k], row=r).wait_recv()

        def send_row(j, k=k):
            buckets[k][j] = landed[k][inv_ref[j]]
            remote(buckets[k].at[j], mirrored[k].at[j], 2, b_sem.at[k], row=lax.rem(r + j, nr)).start()

        def send_rows(s, carry):
            send_row(nr // 2 - s)
            send_row(nr // 2 + s)
            return carry

        send_row(nr // 2)
        lax.fori_loop(1, nr // 2, send_rows, 0)
        if k == 0:
            gather_x()
        if k == min(1, chunks - 1):
            gather_core()
        if k > 0:
            relay_on(k - 1)
        remote(mirrored[k].at[pl.ds(1, nr - 1)], mirrored[k].at[pl.ds(1, nr - 1)], 2, b_sem.at[k], row=r).wait_recv()

        def complete(j, carry, k=k, rows_k=rows_k):
            total[j, rows_k] = stored_ref[inv_ref[j], rows_k] + mirrored[k][j]
            return carry

        lax.fori_loop(1, nr, complete, 0)
        shift_on(k)

    relay_on(chunks - 1)
    plane = gathered.at[:, :, core]
    for s in range(1, ncore):
        remote(plane, plane, 7 + ny + nx + s, g_sem.at[ny + nx + s], row=r).wait_recv()
    shift = jc_ref[following]

    def place(row):
        row = lax.rem(row + 2 * nr, nr)
        return lax.div(row, ncore * nx), lax.rem(lax.div(row, ncore), nx), lax.rem(row, ncore)

    def fill_ahead(p, carry):
        here, there = place(p), place(p - shift)
        ahead[p] = gathered[here[0], here[1], here[2], 1] + gathered[there[0], there[1], there[2], 2]
        return carry

    lax.fori_loop(0, nr, fill_ahead, 0)

    def diag_term(t, carry):
        j = jc_ref[t]
        at = place(r - j)
        out_ref[t] = jnp.dot(total[j], gathered[at[0], at[1], at[2], 0], preferred_element_type=jnp.float32)
        return carry

    lax.fori_loop(0, nc, diag_term, 0, unroll=2)
    for k in range(chunks):
        rows_k = pl.ds(starts[k], strips[k])
        remote(total.at[:, rows_k], total_next.at[:, rows_k], 3, w_sem.at[k], col=previous).wait_recv()

    def ahead_term(t, carry):
        j = lax.rem(jc_ref[t] - shift + nr, nr)
        out_ref[t] += jnp.dot(
            total_next[j], ahead[lax.rem(r - j + nr, nr)], preferred_element_type=jnp.float32
        )
        return carry

    lax.fori_loop(0, nc, ahead_term, 0, unroll=2)

    ahead_copy.wait_send()
    sent = turned.at[pl.ds(0, nc - 1)]
    remote(sent, sent, 1, m_sem.at[0], row=r).wait_send()
    for s in range(1, ny):
        remote(mine, mine, 7 + s, g_sem.at[s], row=r).wait_send()
    line = gathered.at[:, x, core]
    for s in range(1, nx):
        remote(line, line, 7 + ny + s, g_sem.at[ny + s], row=r).wait_send()
    for s in range(1, ncore):
        remote(plane, plane, 7 + ny + nx + s, g_sem.at[ny + nx + s], row=r).wait_send()
    remote(turned.at[pl.ds(1, nr - 1)], turned.at[pl.ds(1, nr - 1)], 2, m_sem.at[0], row=r).wait_send()
    remote(total, total, 3, m_sem.at[0], row=r).wait_send()
    for between, _, slots in parts():
        if between != nz - 1:

            @pl.when(z == between)
            def _(slots=slots):
                remote(relayed.at[slots], relayed.at[slots], 5, m_sem.at[0], row=r).wait_send()


def body(row_split, col_split, strips, crossings, stored, pair_rows, pair_cols, block_owner):
    nr, nc = lax.axis_size("row"), lax.axis_size("col")
    places = pair_rows.shape[-1]
    width = stored.shape[-1]
    chunks = len(strips)
    partner = block_owner[pair_cols[0, 0, :, 0, 0]] // (nc * places)
    jc = lax.rem(lax.axis_index("row") - partner + nr, nr)
    slots = lax.broadcasted_iota(jnp.int32, (nr, nc), 1)
    inv = jnp.sum(jnp.where(jc[None, :] == jnp.arange(nr, dtype=jnp.int32)[:, None], slots, 0), axis=1)
    groups = jax.ShapeDtypeStruct((nc, width, width), jnp.bfloat16)
    vmem = lambda *shape: pltpu.VMEM(shape, jnp.bfloat16)
    smem_spec = pl.BlockSpec(memory_space=pltpu.SMEM)
    vmem_spec = pl.BlockSpec(memory_space=pltpu.VMEM)
    out = pl.pallas_call(
        functools.partial(kernel, row_split, col_split, strips, crossings),
        out_shape=jax.ShapeDtypeStruct((nc, width, width), jnp.float32),
        in_specs=[smem_spec, smem_spec, vmem_spec],
        out_specs=vmem_spec,
        scratch_shapes=[
            vmem(nc, width, width),
            vmem(*row_split, 3, width, width),
            vmem(nr, width, width),
            vmem(nr, width, width),
            vmem(nr, width, width),
            vmem(max(count for _, count in crossings), width, width),
            *[vmem(nc, strip, width) for strip in strips],
            *[vmem(nr, strip, width) for strip in strips],
            *[vmem(nr, strip, width) for strip in strips],
            pltpu.SemaphoreType.DMA((7 + sum(row_split),)),
            pltpu.SemaphoreType.DMA((1,)),
            pltpu.SemaphoreType.DMA((sum(row_split),)),
            pltpu.SemaphoreType.DMA((chunks,)),
            pltpu.SemaphoreType.DMA((chunks,)),
            pltpu.SemaphoreType.DMA((chunks,)),
            pltpu.SemaphoreType.DMA((chunks,)),
        ],
        compiler_params=pltpu.CompilerParams(
            collective_id=0, has_side_effects=True, vmem_limit_bytes=40 * 1024 * 1024
        ),
    )(jc, inv, stored[0, 0])
    return out[None, None]


def build(mesh, row_split, col_split, strips, crossings):
    in_specs = (
        P("row", "col", None, None, None),
        P("row", "col", None, None, None),
        P("row", "col", None, None, None),
        P(),
    )
    out_specs = P("row", "col", None, None, None)
    run = functools.partial(body, row_split, col_split, strips, crossings)
    return jax.shard_map(run, mesh=mesh, in_specs=in_specs, out_specs=out_specs, check_vma=False)


def solution(mesh):
    return build(mesh, ROW_SPLIT, COL_SPLIT, STRIPS, CROSSINGS)
```

```python
import functools

import jax
import jax.numpy as jnp
from jax import lax
from jax.experimental import pallas as pl
from jax.experimental.pallas import tpu as pltpu
from jax.sharding import PartitionSpec as P

MESH = pl.DeviceIdType.MESH

ROW_SPLIT = (4, 4, 2)
COL_SPLIT = (2, 16)
STRIPS = (32, 32, 32, 32)
CROSSINGS = ((15, 7), (14, 5), (13, 5), (12, 5), (11, 5), (10, 5))


def kernel(
    row_split, col_split, strips, crossings, jc_ref, inv_ref, stored_ref, out_ref, turned, gathered, ahead, total, total_next, relayed, *rest
):
    chunks = len(strips)
    starts = [sum(strips[:k]) for k in range(chunks)]
    landed, buckets, mirrored = rest[:chunks], rest[chunks : 2 * chunks], rest[2 * chunks : 3 * chunks]
    send_sem, m_sem, g_sem, a_sem, b_sem, w_sem, r_sem = rest[3 * chunks :]
    ny, nx, ncore = row_split
    nhi, nz = col_split
    nr, nc = ny * nx * ncore, nhi * nz
    width = stored_ref.shape[-1]
    r, c = lax.axis_index("row"), lax.axis_index("col")
    core, x, y = lax.rem(r, ncore), lax.rem(lax.div(r, ncore), nx), lax.div(r, ncore * nx)
    z, hi = lax.rem(c, nz), lax.div(c, nz)
    following, previous = lax.rem(c + 1, nc), lax.rem(c + nc - 1, nc)

    def remote(src, dst, slot, recv, **where):
        return pltpu.make_async_remote_copy(
            src_ref=src,
            dst_ref=dst,
            send_sem=send_sem.at[slot],
            recv_sem=recv,
            device_id=where,
            device_id_type=MESH,
        )

    barrier = pltpu.get_barrier_semaphore()

    def greet_col(t, carry):
        pl.semaphore_signal(barrier, inc=1, device_id={"col": lax.rem(c + t, nc)}, device_id_type=MESH)
        return carry

    def greet_row(t, carry):
        pl.semaphore_signal(barrier, inc=1, device_id={"row": lax.rem(r + t, nr)}, device_id_type=MESH)
        return carry

    lax.fori_loop(1, nc, greet_col, 0)
    lax.fori_loop(1, nr, greet_row, 0)

    def turn(t, carry):
        turned[t] = stored_ref[t].T
        return carry

    lax.fori_loop(0, nc, turn, 0, unroll=2)

    half = width // 2
    rows = lax.broadcasted_iota(jnp.int32, (width, width), 0)
    cols = lax.broadcasted_iota(jnp.int32, (width, width), 1)
    own = stored_ref[c].astype(jnp.float32)
    flipped = turned[c].astype(jnp.float32)
    diagonal = (own + jnp.where((rows >= half) != (cols >= half), flipped, 0.0)).astype(jnp.bfloat16)
    gathered[y, x, core, 0] = diagonal
    gathered[y, x, core, 1] = stored_ref[following]
    total[0] = diagonal

    pl.semaphore_wait(barrier, nc + nr - 2)

    ahead_copy = remote(
        turned.at[previous], gathered.at[y, x, core, 2], 0, m_sem.at[0], col=previous
    )
    ahead_copy.start()

    here, other = hi * nz, (nhi - 1 - hi) * nz
    far = nz // 2

    def send_to(k, to):
        rows_k = pl.ds(starts[k], strips[k])
        remote(turned.at[to, rows_k], landed[k].at[c], 1, a_sem.at[k], col=to).start()

    def send_cols(k):
        up, down = lax.rem(z + far - 1, nz), lax.rem(z + far + 1, nz)
        send_to(k, here + lax.rem(z + far, nz))
        send_to(k, other + lax.rem(z + far, nz))
        send_to(k, here + down)
        send_to(k, here + up)
        send_to(k, other + down)
        send_to(k, other + up)

        def send_pairs(s, carry):
            m = far - s
            up, down = lax.rem(z + m, nz), lax.rem(z + nz - m, nz)
            send_to(k, here + up)
            send_to(k, other + down)
            send_to(k, other + up)
            send_to(k, here + down)
            return carry

        lax.fori_loop(2, far, send_pairs, 0)
        send_to(k, other + z)

    send_cols(0)
    ahead_copy.wait_recv()
    mine = gathered.at[y, x, core]
    for s in range(1, ny):
        remote(mine, mine, 7 + s, g_sem.at[s], row=(lax.rem(y + s, ny) * nx + x) * ncore + core).start()

    for k in range(1, chunks):
        send_cols(k)

    def gather_x():
        for s in range(1, ny):
            remote(mine, mine, 7 + s, g_sem.at[s], row=r).wait_recv()
        line = gathered.at[:, x, core]
        for s in range(1, nx):
            remote(line, line, 7 + ny + s, g_sem.at[ny + s], row=(y * nx + lax.rem(x + s, nx)) * ncore + core).start()

    def gather_core():
        line = gathered.at[:, x, core]
        for s in range(1, nx):
            remote(line, line, 7 + ny + s, g_sem.at[ny + s], row=r).wait_recv()
        plane = gathered.at[:, :, core]
        for s in range(1, ncore):
            remote(plane, plane, 7 + ny + nx + s, g_sem.at[ny + nx + s], row=(y * nx + x) * ncore + lax.rem(core + s, ncore)).start()

    def parts():
        start = 0
        for plane, count in crossings:
            yield plane, pl.ds(start, count), pl.ds(0, count)
            start += count

    def shift_on(k):
        rows_k = pl.ds(starts[k], strips[k])

        @pl.when(z != 0)
        def _():
            remote(total.at[:, rows_k], total_next.at[:, rows_k], 3, w_sem.at[k], col=previous).start()

        @pl.when(z == 0)
        def _():
            for plane, part, slots in parts():
                to = lax.rem(hi + nhi - 1, nhi) * nz + plane
                if plane == nz - 1:
                    dst, sem = total_next.at[part, rows_k], w_sem.at[k]
                else:
                    dst, sem = relayed.at[slots, rows_k], r_sem.at[k]
                remote(total.at[part, rows_k], dst, 3, sem, col=to).start()

    def relay_on(k):
        rows_k = pl.ds(starts[k], strips[k])
        for plane, part, slots in parts():
            if plane != nz - 1:

                @pl.when(z == plane)
                def _(part=part, slots=slots):
                    src, dst = relayed.at[slots, rows_k], total_next.at[part, rows_k]
                    remote(src, src, 3, r_sem.at[k], row=r).wait_recv()
                    remote(src, dst, 5, w_sem.at[k], col=hi * nz + nz - 1).start()

    for k in range(chunks):
        rows_k = pl.ds(starts[k], strips[k])
        remote(landed[k].at[pl.ds(1, nc - 1)], landed[k].at[pl.ds(1, nc - 1)], 1, a_sem.at[k], row=r).wait_recv()

        def send_row(j, k=k):
            buckets[k][j] = landed[k][inv_ref[j]]
            remote(buckets[k].at[j], mirrored[k].at[j], 2, b_sem.at[k], row=lax.rem(r + j, nr)).start()

        def send_rows(s, carry):
            send_row(nr // 2 - s)
            send_row(nr // 2 + s)
            return carry

        send_row(nr // 2)
        lax.fori_loop(1, nr // 2, send_rows, 0)
        if k == 0:
            gather_x()
        if k == min(1, chunks - 1):
            gather_core()
        if k > 0:
            relay_on(k - 1)
        remote(mirrored[k].at[pl.ds(1, nr - 1)], mirrored[k].at[pl.ds(1, nr - 1)], 2, b_sem.at[k], row=r).wait_recv()

        def complete(j, carry, k=k, rows_k=rows_k):
            total[j, rows_k] = stored_ref[inv_ref[j], rows_k] + mirrored[k][j]
            return carry

        lax.fori_loop(1, nr, complete, 0)
        shift_on(k)

    relay_on(chunks - 1)
    plane = gathered.at[:, :, core]
    for s in range(1, ncore):
        remote(plane, plane, 7 + ny + nx + s, g_sem.at[ny + nx + s], row=r).wait_recv()
    shift = jc_ref[following]

    def place(row):
        row = lax.rem(row + 2 * nr, nr)
        return lax.div(row, ncore * nx), lax.rem(lax.div(row, ncore), nx), lax.rem(row, ncore)

    def fill_ahead(p, carry):
        here, there = place(p), place(p - shift)
        ahead[p] = gathered[here[0], here[1], here[2], 1] + gathered[there[0], there[1], there[2], 2]
        return carry

    lax.fori_loop(0, nr, fill_ahead, 0)

    def diag_term(t, carry):
        j = jc_ref[t]
        at = place(r - j)
        out_ref[t] = jnp.dot(total[j], gathered[at[0], at[1], at[2], 0], preferred_element_type=jnp.float32)
        return carry

    lax.fori_loop(0, nc, diag_term, 0, unroll=2)
    for k in range(chunks):
        rows_k = pl.ds(starts[k], strips[k])
        remote(total.at[:, rows_k], total_next.at[:, rows_k], 3, w_sem.at[k], col=previous).wait_recv()

    def ahead_term(t, carry):
        j = lax.rem(jc_ref[t] - shift + nr, nr)
        out_ref[t] += jnp.dot(
            total_next[j], ahead[lax.rem(r - j + nr, nr)], preferred_element_type=jnp.float32
        )
        return carry

    lax.fori_loop(0, nc, ahead_term, 0, unroll=2)

    ahead_copy.wait_send()
    sent = turned.at[pl.ds(0, nc - 1)]
    remote(sent, sent, 1, m_sem.at[0], row=r).wait_send()
    for s in range(1, ny):
        remote(mine, mine, 7 + s, g_sem.at[s], row=r).wait_send()
    line = gathered.at[:, x, core]
    for s in range(1, nx):
        remote(line, line, 7 + ny + s, g_sem.at[ny + s], row=r).wait_send()
    for s in range(1, ncore):
        remote(plane, plane, 7 + ny + nx + s, g_sem.at[ny + nx + s], row=r).wait_send()
    remote(turned.at[pl.ds(1, nr - 1)], turned.at[pl.ds(1, nr - 1)], 2, m_sem.at[0], row=r).wait_send()
    remote(total, total, 3, m_sem.at[0], row=r).wait_send()
    for between, _, slots in parts():
        if between != nz - 1:

            @pl.when(z == between)
            def _(slots=slots):
                remote(relayed.at[slots], relayed.at[slots], 5, m_sem.at[0], row=r).wait_send()


def body(row_split, col_split, strips, crossings, stored, pair_rows, pair_cols, block_owner):
    nr, nc = lax.axis_size("row"), lax.axis_size("col")
    places = pair_rows.shape[-1]
    width = stored.shape[-1]
    chunks = len(strips)
    partner = block_owner[pair_cols[0, 0, :, 0, 0]] // (nc * places)
    jc = lax.rem(lax.axis_index("row") - partner + nr, nr)
    slots = lax.broadcasted_iota(jnp.int32, (nr, nc), 1)
    inv = jnp.sum(jnp.where(jc[None, :] == jnp.arange(nr, dtype=jnp.int32)[:, None], slots, 0), axis=1)
    groups = jax.ShapeDtypeStruct((nc, width, width), jnp.bfloat16)
    vmem = lambda *shape: pltpu.VMEM(shape, jnp.bfloat16)
    smem_spec = pl.BlockSpec(memory_space=pltpu.SMEM)
    vmem_spec = pl.BlockSpec(memory_space=pltpu.VMEM)
    out = pl.pallas_call(
        functools.partial(kernel, row_split, col_split, strips, crossings),
        out_shape=jax.ShapeDtypeStruct((nc, width, width), jnp.float32),
        in_specs=[smem_spec, smem_spec, vmem_spec],
        out_specs=vmem_spec,
        scratch_shapes=[
            vmem(nc, width, width),
            vmem(*row_split, 3, width, width),
            vmem(nr, width, width),
            vmem(nr, width, width),
            vmem(nr, width, width),
            vmem(max(count for _, count in crossings), width, width),
            *[vmem(nc, strip, width) for strip in strips],
            *[vmem(nr, strip, width) for strip in strips],
            *[vmem(nr, strip, width) for strip in strips],
            pltpu.SemaphoreType.DMA((7 + sum(row_split),)),
            pltpu.SemaphoreType.DMA((1,)),
            pltpu.SemaphoreType.DMA((sum(row_split),)),
            pltpu.SemaphoreType.DMA((chunks,)),
            pltpu.SemaphoreType.DMA((chunks,)),
            pltpu.SemaphoreType.DMA((chunks,)),
            pltpu.SemaphoreType.DMA((chunks,)),
        ],
        compiler_params=pltpu.CompilerParams(
            collective_id=0, has_side_effects=True, vmem_limit_bytes=40 * 1024 * 1024
        ),
    )(jc, inv, stored[0, 0])
    return out[None, None]


def build(mesh, row_split, col_split, strips, crossings):
    in_specs = (
        P("row", "col", None, None, None),
        P("row", "col", None, None, None),
        P("row", "col", None, None, None),
        P(),
    )
    out_specs = P("row", "col", None, None, None)
    run = functools.partial(body, row_split, col_split, strips, crossings)
    return jax.shard_map(run, mesh=mesh, in_specs=in_specs, out_specs=out_specs, check_vma=False)


def solution(mesh):
    return build(mesh, ROW_SPLIT, COL_SPLIT, STRIPS, CROSSINGS)
```
